32 devices in a mesh: dp: 8 (over z, x), seq: 4 (over y, core).
Axes of the slice: x: 2, y: 2, z: 4, core: 2. Of those that a mesh axis runs over, the one named last changes fastest.
Arguments:
- tokens: bfloat16 [8, 512, 1024], P('dp', 'seq'), may hold values from -6 to 6
- cotangent: bfloat16 [8, 512, 2048], P('dp', 'seq'), may hold values from -6 to 6
- input_weight: bfloat16 [1024, 4096], P('dp'), may hold values from -0.1875 to 0.1875
- filter_weight: float32 [2, 4, 2048], P(None, None, 'dp'), may hold values from -3 to 3
- filter_bias: float32 [2, 2048], P(None, 'dp'), may hold values from -0.5 to 0.5
- scan_weight: float32 [2, 2048, 96], P(None, 'dp'), may hold values from -0.125 to 0.125
- step_weight: float32 [2, 64, 2048], P(None, None, 'dp'), may hold values from -0.75 to 0.75
- step_bias: float32 [2, 2048], P(None, 'dp'), may hold values from -6 to -2.5
- log_rate: float32 [2, 16, 2048], P(None, None, 'dp'), may hold values from -4 to 1
- skip_gain: float32 [2, 2048], P(None, 'dp'), may hold values from 0.5 to 1.5
Outputs:
- mixed: bfloat16 [8, 512, 2048], P('dp', 'seq')
- tokens_gradient: bfloat16 [8, 512, 1024], P('dp', 'seq')
- input_weight_gradient: float32 [1024, 4096], P(('dp', 'seq'))
- filter_weight_gradient: float32 [2, 4, 2048], P(None, None, ('dp', 'seq'))
- filter_bias_gradient: float32 [2, 2048], P(None, ('dp', 'seq'))
- scan_weight_gradient: float32 [2, 2048, 96], P(None, ('dp', 'seq'))
- step_weight_gradient: float32 [2, 64, 2048], P(None, None, ('dp', 'seq'))
- step_bias_gradient: float32 [2, 2048], P(None, ('dp', 'seq'))
- log_rate_gradient: float32 [2, 16, 2048], P(None, None, ('dp', 'seq'))
- skip_gain_gradient: float32 [2, 2048], P(None, ('dp', 'seq'))
The draws below stay inside these ranges and needn't reach their ends.
All inputs are finite; a program needn't handle non-finite values.
Results may differ from the reference program's by a relative error of at most 0.0072.
Values may be sent and summed in bfloat16 or wider, within the bound.
A program may use at most 128 MiB of HBM per device.

```python
import jax
import jax.numpy as jnp
from jax import lax

D = 1024
E = 2048
N = 16
K = 4
R = 64
BLOCK = 8
LENGTH = 512
SEQS = 8


def level_of(stream_key, shape, split, least, largest):
    level, own = 1.0, jax.random.fold_in(stream_key, 6)
    for dim, blocks in split:
        heights = jnp.exp(jax.random.uniform(jax.random.fold_in(own, dim), (blocks,), jnp.float32, least / len(split), largest / len(split)))
        level = level * jnp.repeat(heights, shape[dim] // blocks).reshape([-1 if axis == dim else 1 for axis in range(len(shape))])
    return level


def bell_draw(key, shape, spread, limit, shards=(), dtype=jnp.bfloat16):
    entries = jax.random.normal(key, shape, jnp.float32) * spread
    if len(shards) > 0:
        entries = level_of(key, shape, shards, -0.22, 0.18) * entries
    return jnp.clip(entries, min=-limit, max=limit).astype(dtype)


def setup_inputs(seed: int = 0) -> dict:
    streams_of = jax.random.split(jax.random.key(seed), 11)
    tokens = bell_draw(streams_of[0], (SEQS, LENGTH, D), 1.0, 6.0, ((0, 8), (1, 4)))
    cotangent = bell_draw(streams_of[1], (SEQS, LENGTH, E), 1.0, 6.0, ((0, 8), (1, 4)))
    input_weight = bell_draw(streams_of[2], (D, 2 * E), D ** -0.5, 0.1875, ((0, 8),))
    filter_weight = bell_draw(streams_of[3], (2, K, E), K ** -0.5, 3.0, ((2, 8),), jnp.float32)
    filter_bias = jnp.clip(jax.random.uniform(streams_of[4], (2, E), jnp.float32, -0.5, 0.5) * level_of(streams_of[4], (2, E), ((1, 8),), -0.4, 0.0), -0.5, 0.5)
    scan_weight = bell_draw(streams_of[5], (2, E, R + 2 * N), E ** -0.5, 0.125, ((1, 8),), jnp.float32)
    step_weight = bell_draw(streams_of[6], (2, R, E), R ** -0.5, 0.75, ((2, 8),), jnp.float32)
    step_bias = jnp.clip(-6.0 + 3.5 * jax.random.uniform(streams_of[7], (2, E), jnp.float32) ** level_of(streams_of[7], (2, E), ((1, 8),), -0.2, 0.2), -6.0, -2.5)
    log_rate = jnp.clip(-4.0 + 5.0 * jax.random.uniform(streams_of[8], (2, N, E), jnp.float32) ** level_of(streams_of[8], (2, N, E), ((2, 8),), -0.2, 0.2), -4.0, 1.0)
    skip_gain = jnp.clip(0.5 + 1.0 * jax.random.uniform(streams_of[9], (2, E), jnp.float32) ** level_of(streams_of[9], (2, E), ((1, 8),), -0.2, 0.2), 0.5, 1.5)
    return dict(tokens=tokens, cotangent=cotangent, input_weight=input_weight, filter_weight=filter_weight, filter_bias=filter_bias, scan_weight=scan_weight, step_weight=step_weight, step_bias=step_bias, log_rate=log_rate, skip_gain=skip_gain)


HIGH = lax.Precision.HIGHEST

def block_scan(state_in, active, steps, inputs, reads, log_rate, skip_gain):
    rate = -jnp.exp(log_rate)
    length = active.shape[0]
    count = length // BLOCK

    def advance(state, block):
        active_part, step_part, input_part, read_part = block
        drive_part = step_part * active_part
        results = []
        for place in range(BLOCK):
            state = jnp.exp(step_part[place][None] * rate) * state + drive_part[place][None] * input_part[place][:, None]
            results.append(jnp.dot(read_part[place], state, precision=HIGH))
        result = jnp.stack(results) + skip_gain * active_part
        return (state, result)
    blocks = tuple((array.reshape(count, BLOCK, array.shape[1]) for array in (active, steps, inputs, reads)))
    state_out, results = lax.scan(jax.checkpoint(advance), state_in, blocks)
    return (results.reshape(length, active.shape[1]), state_out)

def prepare(padded, filter_weight, filter_bias, scan_weight, step_weight, step_bias, which):
    length = padded.shape[0] - 2 * (K - 1)
    filtered = filter_bias[which]
    for tap in range(K):
        start = tap if which == 0 else 2 * (K - 1) - tap
        filtered = filtered + filter_weight[which, tap] * padded[start:start + length]
    active = jax.nn.silu(filtered)
    coefficients = jnp.dot(active, scan_weight[which], precision=HIGH)
    steps = jax.nn.softplus(jnp.dot(coefficients[:, :R], step_weight[which], precision=HIGH) + step_bias[which])
    return (active, steps, coefficients[:, R:R + N], coefficients[:, R + N:])

def mixer(projected, filter_weight, filter_bias, scan_weight, step_weight, step_bias, log_rate, skip_gain):
    whole = projected.astype(jnp.float32)
    values = whole[:, :E]
    gates = whole[:, E:]
    padded = jnp.pad(values, ((K - 1, K - 1), (0, 0)))
    total = jnp.zeros(values.shape, jnp.float32)
    for which in range(2):
        prepared = prepare(padded, filter_weight, filter_bias, scan_weight, step_weight, step_bias, which)
        if which == 1:
            prepared = tuple((array[::-1] for array in prepared))
        zero_state = jnp.zeros((N, E), jnp.float32)
        output, _ = block_scan(zero_state, prepared[0], prepared[1], prepared[2], prepared[3], log_rate[which], skip_gain[which])
        if which == 1:
            output = output[::-1]
        total = total + output
    return total * jax.nn.silu(gates)

def reference(tokens, cotangent, input_weight, filter_weight, filter_bias, scan_weight, step_weight, step_bias, log_rate, skip_gain):
    params = (filter_weight, filter_bias, scan_weight, step_weight, step_bias, log_rate, skip_gain)

    def one_sequence(carry, pair):
        sequence, tangent = pair
        projected = jnp.dot(sequence, input_weight, preferred_element_type=jnp.float32).astype(jnp.bfloat16)
        result, pullback = jax.vjp(mixer, projected, filter_weight, filter_bias, scan_weight, step_weight, step_bias, log_rate, skip_gain)
        backs = pullback(tangent.astype(jnp.float32))
        back_projected = backs[0]
        tokens_back = jnp.dot(back_projected, input_weight.T, preferred_element_type=jnp.float32).astype(jnp.bfloat16)
        weight_back = lax.dot_general(sequence, back_projected, (((0,), (0,)), ((), ())), preferred_element_type=jnp.float32)
        updated = (carry[0] + weight_back,) + tuple((carry[index + 1] + backs[index + 1] for index in range(7)))
        return (updated, (result.astype(jnp.bfloat16), tokens_back))
    start = (jnp.zeros(input_weight.shape, jnp.float32),) + tuple((jnp.zeros(param.shape, jnp.float32) for param in params))
    sums, outputs = lax.scan(one_sequence, start, (tokens, cotangent))
    return (outputs[0], outputs[1], sums[0], sums[1], sums[2], sums[3], sums[4], sums[5], sums[6], sums[7])
```

```python
from functools import partial

import jax
import jax.numpy as jnp
from jax import lax
from jax.sharding import PartitionSpec as P

N = 16
K = 4
R = 64
BLOCK = 8


HIGH = lax.Precision.HIGHEST


def extended(x, sides, width):
    for axis, dim in sides:
        peers, length = (lax.axis_size(axis), x.shape[dim])
        up = [(i, (i + 1) % peers) for i in range(peers - 1)]
        down = [(j, i) for i, j in up]
        last = lax.slice_in_dim(x, length - width, length, axis=dim)
        first = lax.slice_in_dim(x, 0, width, axis=dim)
        before = lax.ppermute(last, axis, up)
        after = lax.ppermute(first, axis, down)
        x = jnp.concatenate([before, x, after], axis=dim)
    return x


def block_scan(state_in, active, steps, inputs, reads, log_rate, skip_gain):
    rate = -jnp.exp(log_rate)
    length = active.shape[0]
    count = length // BLOCK

    def block_advance(state, block):
        active_part, step_part, input_part, read_part = block
        drive_part = step_part * active_part
        results = []
        for place in range(BLOCK):
            state = (
                jnp.exp(step_part[place][None] * rate) * state
                + drive_part[place][None] * input_part[place][:, None]
            )
            results.append(jnp.dot(read_part[place], state, precision=HIGH))
        result = jnp.stack(results) + skip_gain * active_part
        return (state, result)

    blocks = tuple(
        (array.reshape(count, BLOCK, array.shape[1]) for array in (active, steps, inputs, reads))
    )
    state_out, results = lax.scan(jax.checkpoint(block_advance), state_in, blocks)
    return (results.reshape(length, active.shape[1]), state_out)


def prepare(padded, filter_weight, filter_bias, scan_weight, step_weight, step_bias, which):
    length = padded.shape[0] - 2 * (K - 1)
    filtered = filter_bias[which]
    for tap in range(K):
        start = tap if which == 0 else 2 * (K - 1) - tap
        filtered = filtered + filter_weight[which, tap] * padded[start : start + length]
    active = jax.nn.silu(filtered)
    coefficients = jnp.dot(active, scan_weight[which], precision=HIGH)
    steps = jax.nn.softplus(
        jnp.dot(coefficients[:, :R], step_weight[which], precision=HIGH) + step_bias[which]
    )
    return (active, steps, coefficients[:, R : R + N], coefficients[:, R + N :])


def forward_summary(active, steps, inputs, log_rate):
    rate = -jnp.exp(log_rate)
    count = active.shape[0] // BLOCK

    def forward_advance(carry, block):
        state, elapsed = carry
        active_part, step_part, input_part = block
        within = jnp.cumsum(step_part, axis=0)
        span = within[-1]
        weights = (
            jnp.exp((span[None] - within)[:, None, :] * rate[None])
            * (step_part * active_part)[:, None, :]
        )
        local = jnp.einsum("qn,qne->ne", input_part, weights, precision=HIGH)
        return ((jnp.exp(span[None] * rate) * state + local, elapsed + span), None)

    blocks = tuple(
        (array.reshape(count, BLOCK, array.shape[1]) for array in (active, steps, inputs))
    )
    start = (jnp.zeros(rate.shape, jnp.float32), jnp.zeros(rate.shape[1:], jnp.float32))
    (state, elapsed), _ = lax.scan(forward_advance, start, blocks)
    return (jnp.exp(elapsed[None] * rate), state)


def adjoint_summary(steps, reads, back_out, log_rate):
    rate = -jnp.exp(log_rate)
    count = steps.shape[0] // BLOCK

    def adjoint_advance(elapsed, block):
        step_part, read_part, back_part = block
        within = elapsed[None] + jnp.cumsum(step_part, axis=0)
        weights = jnp.exp(within[:, None, :] * rate[None]) * back_part[:, None, :]
        return (within[-1], jnp.einsum("qn,qne->ne", read_part, weights, precision=HIGH))

    blocks = tuple(
        (array.reshape(count, BLOCK, array.shape[1]) for array in (steps, reads, back_out))
    )
    _, parts = lax.scan(adjoint_advance, jnp.zeros(steps.shape[1:], jnp.float32), blocks)
    return jnp.sum(parts, axis=0)


def chain(decays, states, reverse):
    count = lax.axis_size("seq")
    place = lax.axis_index("seq")
    ahead = count - 1 - place if reverse else place
    state = jnp.zeros_like(states[0])
    for step in range(count - 1):
        source = count - 1 - step if reverse else step
        state = jnp.where(step < ahead, decays[source] * state + states[source], state)
    return state


def pack_rows(arrays, multiple):
    fw, fb, sw, tw, tb, lr, sg = arrays
    channels = fb.shape[1]
    rows = [fw, fb, sw.transpose(0, 2, 1), tw, tb, lr, sg]
    rows = [row.reshape(-1, channels) for row in rows]
    used = sum(row.shape[0] for row in rows)
    pad = -used % multiple
    return jnp.concatenate(rows + [jnp.zeros((pad, channels), jnp.float32)], axis=0)


def unpack_rows(packed):
    channels = packed.shape[1]
    sizes = (2 * K, 2, 2 * (R + 2 * N), 2 * R, 2, 2 * N, 2)
    parts = []
    start = 0
    for size in sizes:
        parts.append(packed[start : start + size])
        start += size
    return (
        parts[0].reshape(2, K, channels),
        parts[1],
        parts[2].reshape(2, R + 2 * N, channels).transpose(0, 2, 1),
        parts[3].reshape(2, R, channels),
        parts[4],
        parts[5].reshape(2, N, channels),
        parts[6],
    )


def shards(
    tokens,
    cotangent,
    input_weight,
    filter_weight,
    filter_bias,
    scan_weight,
    step_weight,
    step_bias,
    log_rate,
    skip_gain,
):
    full_weight = lax.all_gather(input_weight, "dp", axis=0, tiled=True)
    packed = pack_rows(
        (filter_weight, filter_bias, scan_weight, step_weight, step_bias, log_rate, skip_gain), 8
    )
    spread = lax.all_gather(packed, "dp", axis=0)
    params = unpack_rows(spread.transpose(1, 0, 2).reshape(packed.shape[0], -1))
    all_tokens = lax.all_gather(tokens[0], "seq", axis=0, tiled=True)
    inputs = tokens[0]
    projected = jnp.dot(inputs, full_weight, preferred_element_type=jnp.float32).astype(
        jnp.bfloat16
    )
    width = projected.shape[1] // 2
    rim = K - 1
    widened = extended(projected[:, :width], (("seq", 0),), rim)
    padded = widened.astype(jnp.float32)
    gates = projected[:, width:].astype(jnp.float32)
    prepared_list = []
    prep_pulls = []
    summaries = []
    for which in range(2):
        prepared, prep_pull = jax.vjp(
            partial(prepare, which=which),
            padded,
            params[0],
            params[1],
            params[2],
            params[3],
            params[4],
        )
        if which == 1:
            prepared = tuple((array[::-1] for array in prepared))
        prepared_list.append(prepared)
        prep_pulls.append(prep_pull)
        summaries.append(forward_summary(prepared[0], prepared[1], prepared[2], params[5][which]))
    told = lax.all_gather(jnp.stack([part for pair in summaries for part in pair]), "seq", axis=0)
    start_rise = chain(told[:, 0], told[:, 1], False)
    start_fall = chain(told[:, 2], told[:, 3], True)
    starts = (start_rise, start_fall)
    outputs = []
    scan_pulls = []
    for which in range(2):
        active, steps, inputs_coef, reads = prepared_list[which]
        result, scan_pull = jax.vjp(
            block_scan,
            starts[which],
            active,
            steps,
            inputs_coef,
            reads,
            params[5][which],
            params[6][which],
        )
        outputs.append(result[0])
        scan_pulls.append(scan_pull)
    total = outputs[0] + outputs[1][::-1]
    gate, gate_pull = jax.vjp(jax.nn.silu, gates)
    mixed = (total * gate).astype(jnp.bfloat16)
    tangent = cotangent[0].astype(jnp.float32)
    back_total = tangent * gate
    back_gates = gate_pull(tangent * total)[0]
    directed = (back_total, back_total[::-1])
    flows = []
    for which in range(2):
        flows.append(
            adjoint_summary(
                prepared_list[which][1], prepared_list[which][3], directed[which], params[5][which]
            )
        )
    late_told = lax.all_gather(jnp.stack(flows), "seq", axis=0)
    late_one = chain(told[:, 2], late_told[:, 1], False)
    late_zero = chain(told[:, 0], late_told[:, 0], True)
    lates = (late_zero, late_one)
    back_padded = jnp.zeros_like(padded)
    param_backs = [jnp.zeros_like(param) for param in params[:5]]
    rate_rows = []
    skip_rows = []
    for which in range(2):
        backs = scan_pulls[which]((directed[which], lates[which]))
        prep_backs = backs[1:5]
        if which == 1:
            prep_backs = tuple((array[::-1] for array in prep_backs))
        more = prep_pulls[which](prep_backs)
        back_padded = back_padded + more[0]
        param_backs = [older + newer for older, newer in zip(param_backs, more[1:])]
        rate_rows.append(backs[5])
        skip_rows.append(backs[6])
    rims = jnp.concatenate([back_padded[:rim], back_padded[-rim:]], axis=0)
    returned = extended(rims, (("seq", 0),), rim)
    middle = back_padded[rim:-rim]
    back_values = jnp.concatenate(
        [middle[:rim] + returned[:rim], middle[rim:-rim], middle[-rim:] + returned[-rim:]], axis=0
    )
    back_projected = jnp.concatenate([back_values, back_gates], axis=1).astype(jnp.bfloat16)
    tokens_back = lax.dot_general(
        back_projected, full_weight, (((1,), (1,)), ((), ())), preferred_element_type=jnp.float32
    ).astype(jnp.bfloat16)
    groups, peers = lax.axis_size("dp"), lax.axis_size("seq")
    all_back = lax.all_gather(back_projected, "seq", axis=0, tiled=True)
    depth = all_tokens.shape[1]
    shared = all_tokens.reshape(all_tokens.shape[0], groups, peers, depth // (groups * peers))
    mine = lax.dynamic_index_in_dim(shared, lax.axis_index("seq"), 2, False)
    weight_back = lax.dot_general(
        mine.reshape(mine.shape[0], -1),
        all_back,
        (((0,), (0,)), ((), ())),
        preferred_element_type=jnp.float32,
    ).astype(jnp.bfloat16)
    wide = weight_back.shape[1]
    weight_back = weight_back.reshape(groups, -1, wide)
    rates_back = jnp.stack(rate_rows)
    skip_back = jnp.stack(skip_rows)
    own = skip_back.shape[1] // (groups * peers)
    small = pack_rows((*param_backs, rates_back, skip_back), wide // own).astype(jnp.bfloat16)
    height = small.shape[0]
    small = small.reshape(height, groups, peers, own).transpose(2, 1, 0, 3)
    small = lax.all_to_all(small.reshape(peers, groups, -1, wide), "seq", 0, 0)
    small = jnp.sum(small.astype(jnp.float32), axis=0).astype(jnp.bfloat16)
    joined = jnp.concatenate([weight_back, small], axis=1)
    joined = lax.all_to_all(joined, "dp", 0, 0)
    joined = jnp.sum(joined.astype(jnp.float32), axis=0)
    edge = weight_back.shape[1]
    sums = (joined[:edge], *unpack_rows(joined[edge:].reshape(height, own)))
    return (
        mixed[None],
        tokens_back[None],
        sums[0],
        sums[1],
        sums[2],
        sums[3],
        sums[4],
        sums[5],
        sums[6],
        sums[7],
    )


def solution(mesh):
    in_specs = (
        P("dp", "seq", None),
        P("dp", "seq", None),
        P("dp", None),
        P(None, None, "dp"),
        P(None, "dp"),
        P(None, "dp", None),
        P(None, None, "dp"),
        P(None, "dp"),
        P(None, None, "dp"),
        P(None, "dp"),
    )
    out_specs = (
        P("dp", "seq", None),
        P("dp", "seq", None),
        P(("dp", "seq"), None),
        P(None, None, ("dp", "seq")),
        P(None, ("dp", "seq")),
        P(None, ("dp", "seq"), None),
        P(None, None, ("dp", "seq")),
        P(None, ("dp", "seq")),
        P(None, None, ("dp", "seq")),
        P(None, ("dp", "seq")),
    )
    return jax.shard_map(shards, mesh=mesh, in_specs=in_specs, out_specs=out_specs, check_vma=False)
```

```python
from functools import partial

import jax
import jax.numpy as jnp
from jax import lax
from jax.experimental import pallas as pl
from jax.experimental.pallas import tpu as pltpu
from jax.sharding import PartitionSpec as P

N = 16
K = 4
R = 64


HIGH = lax.Precision.HIGHEST


def extended(x, sides, width):
    for axis, dim in sides:
        peers, length = (lax.axis_size(axis), x.shape[dim])
        up = [(i, (i + 1) % peers) for i in range(peers - 1)]
        down = [(j, i) for i, j in up]
        last = lax.slice_in_dim(x, length - width, length, axis=dim)
        first = lax.slice_in_dim(x, 0, width, axis=dim)
        before = lax.ppermute(last, axis, up)
        after = lax.ppermute(first, axis, down)
        x = jnp.concatenate([before, x, after], axis=dim)
    return x


def prepare(padded, filter_weight, filter_bias, scan_weight, step_weight, step_bias, which):
    length = padded.shape[0] - 2 * (K - 1)
    filtered = filter_bias[which]
    for tap in range(K):
        start = tap if which == 0 else 2 * (K - 1) - tap
        filtered = filtered + filter_weight[which, tap] * padded[start : start + length]
    active = jax.nn.silu(filtered)
    coefficients = jnp.dot(active, scan_weight[which], precision=HIGH)
    steps = jax.nn.softplus(
        jnp.dot(coefficients[:, :R], step_weight[which], precision=HIGH) + step_bias[which]
    )
    return (active, steps, coefficients[:, R : R + N], coefficients[:, R + N :])


LANES = 128
TILE = 512
UNROLL = 4
LIMIT = 48 * 1024 * 1024


def row_of(ref, at):
    return ref[0, pl.ds(at, 1), :]


def summary_kernel(active, steps, back, inputs, reads, rate, state_out, flow_out, span_out):
    length = active.shape[1]
    falling = pl.program_id(0)
    repeat = rate.shape[2] // LANES
    rates = rate[0]

    def wide(ref, at):
        return jnp.concatenate([ref[0, at]] * repeat, axis=1)

    def place_of(t):
        return t + falling * (length - 1 - 2 * t)

    def one(t, carry):
        state, flow, span = carry
        at = place_of(t)
        step = row_of(steps, at)
        state = jnp.exp(step * rates) * state + (step * row_of(active, at)) * wide(inputs, at)
        end = place_of(length - 1 - t)
        flow = flow + row_of(back, end) * wide(reads, end)
        flow = jnp.exp(row_of(steps, end) * rates) * flow
        return (state, flow, span + step)

    zero = jnp.zeros(rates.shape, jnp.float32)
    start = (zero, zero, jnp.zeros((1, rates.shape[1]), jnp.float32))
    state, flow, span = lax.fori_loop(0, length, one, start, unroll=UNROLL)
    state_out[0] = state
    flow_out[0] = flow
    span_out[0] = jnp.exp(span * rates)


def scan_kernel(
    active, steps, back, inputs, reads, rate, skip, first, late,
    result, active_back, steps_back, inputs_back, reads_back, rate_back, skip_back, held,
):
    length = active.shape[1]
    falling = pl.program_id(0)
    repeat = rate.shape[2] // LANES
    rates = rate[0]
    gain = skip[0]

    def wide(ref, at):
        return jnp.concatenate([ref[0, at]] * repeat, axis=1)

    def narrow(x):
        return sum(x[:, i * LANES : (i + 1) * LANES] for i in range(repeat))

    def place_of(t):
        return t + falling * (length - 1 - 2 * t)

    @pl.when(pl.program_id(1) == 0)
    def _():
        inputs_back[...] = jnp.zeros_like(inputs_back)
        reads_back[...] = jnp.zeros_like(reads_back)

    held[0] = first[0]

    def forward(t, state):
        at = place_of(t)
        step = row_of(steps, at)
        act = row_of(active, at)
        state = jnp.exp(step * rates) * state + (step * act) * wide(inputs, at)
        held[t + 1] = state
        out = jnp.sum(wide(reads, at) * state, axis=0, keepdims=True)
        result[0, pl.ds(at, 1), :] = out + gain * act
        return state

    lax.fori_loop(0, length, forward, first[0], unroll=UNROLL)

    def backward(i, carry):
        adjoint, rate_sum, skip_sum = carry
        t = length - 1 - i
        at = place_of(t)
        step = row_of(steps, at)
        act = row_of(active, at)
        grad = row_of(back, at)
        adjoint = adjoint + grad * wide(reads, at)
        reads_back[0, at] += narrow(grad * held[t + 1])
        passed = jnp.exp(step * rates) * adjoint
        decay_back = passed * held[t]
        inputs_back[0, at] += narrow(adjoint * (step * act))
        drive_back = jnp.sum(adjoint * wide(inputs, at), axis=0, keepdims=True)
        steps_back[0, pl.ds(at, 1), :] = (
            jnp.sum(decay_back * rates, axis=0, keepdims=True) + act * drive_back
        )
        active_back[0, pl.ds(at, 1), :] = step * drive_back + gain * grad
        return (passed, rate_sum + decay_back * step, skip_sum + grad * act)

    start = (late[0], jnp.zeros_like(rates), jnp.zeros_like(gain))
    _, rate_sum, skip_sum = lax.fori_loop(0, length, backward, start, unroll=UNROLL)
    rate_back[0] = rate_sum * rates
    skip_back[0] = skip_sum


def specs_of(length, tile):
    rows = pl.BlockSpec((1, length, tile), lambda d, c: (d, 0, c))
    shared = pl.BlockSpec((1, length, tile), lambda d, c: (0, 0, c))
    spread = pl.BlockSpec((1, length, N, LANES), lambda d, c: (d, 0, 0, 0))
    state = pl.BlockSpec((1, N, tile), lambda d, c: (d, 0, c))
    single = pl.BlockSpec((1, 1, tile), lambda d, c: (d, 0, c))
    return (rows, shared, spread, state, single)


def summarise(active, steps, back, inputs, reads, rate):
    _, length, channels = active.shape
    tile = min(TILE, channels)
    rows, shared, spread, state, _ = specs_of(length, tile)
    return pl.pallas_call(
        summary_kernel,
        grid=(2, channels // tile),
        in_specs=[rows, rows, shared, spread, spread, state],
        out_specs=[state, state, state],
        out_shape=[jax.ShapeDtypeStruct(rate.shape, jnp.float32)] * 3,
        compiler_params=pltpu.CompilerParams(vmem_limit_bytes=LIMIT),
    )(active, steps, back, inputs, reads, rate)


def scan_all(active, steps, back, inputs, reads, rate, skip, first, late):
    _, length, channels = active.shape
    tile = min(TILE, channels)
    rows, shared, spread, state, single = specs_of(length, tile)
    full = jax.ShapeDtypeStruct(active.shape, jnp.float32)
    narrow = jax.ShapeDtypeStruct(inputs.shape, jnp.float32)
    return pl.pallas_call(
        scan_kernel,
        grid=(2, channels // tile),
        in_specs=[rows, rows, shared, spread, spread, state, single, state, state],
        out_specs=[rows, rows, rows, spread, spread, state, single],
        out_shape=[
            full, full, full, narrow, narrow,
            jax.ShapeDtypeStruct(rate.shape, jnp.float32),
            jax.ShapeDtypeStruct(skip.shape, jnp.float32),
        ],
        scratch_shapes=[pltpu.VMEM((length + 1, N, tile), jnp.float32)],
        compiler_params=pltpu.CompilerParams(vmem_limit_bytes=LIMIT),
    )(active, steps, back, inputs, reads, rate, skip, first, late)


def chain(decays, states, reverse):
    count = lax.axis_size("seq")
    place = lax.axis_index("seq")
    ahead = count - 1 - place if reverse else place
    state = jnp.zeros_like(states[0])
    for step in range(count - 1):
        source = count - 1 - step if reverse else step
        state = jnp.where(step < ahead, decays[source] * state + states[source], state)
    return state


def pack_rows(arrays, multiple):
    fw, fb, sw, tw, tb, lr, sg = arrays
    channels = fb.shape[1]
    rows = [fw, fb, sw.transpose(0, 2, 1), tw, tb, lr, sg]
    rows = [row.reshape(-1, channels) for row in rows]
    used = sum(row.shape[0] for row in rows)
    pad = -used % multiple
    return jnp.concatenate(rows + [jnp.zeros((pad, channels), jnp.float32)], axis=0)


def unpack_rows(packed):
    channels = packed.shape[1]
    sizes = (2 * K, 2, 2 * (R + 2 * N), 2 * R, 2, 2 * N, 2)
    parts = []
    start = 0
    for size in sizes:
        parts.append(packed[start : start + size])
        start += size
    return (
        parts[0].reshape(2, K, channels),
        parts[1],
        parts[2].reshape(2, R + 2 * N, channels).transpose(0, 2, 1),
        parts[3].reshape(2, R, channels),
        parts[4],
        parts[5].reshape(2, N, channels),
        parts[6],
    )


def spread_rows(block):
    share = block.shape[0] // lax.axis_size("seq")
    part = lax.dynamic_slice_in_dim(block, lax.axis_index("seq") * share, share, axis=0)
    part = lax.all_gather(part, "dp", axis=0)
    parts = lax.all_gather(part, "seq", axis=0)
    return parts.transpose(1, 0, 2, 3).reshape(parts.shape[1], -1, block.shape[1])


def shards(
    tokens,
    cotangent,
    input_weight,
    filter_weight,
    filter_bias,
    scan_weight,
    step_weight,
    step_bias,
    log_rate,
    skip_gain,
):
    full_weight = spread_rows(input_weight)
    full_weight = full_weight.reshape(-1, input_weight.shape[1])
    packed = pack_rows(
        (filter_weight, filter_bias, scan_weight, step_weight, step_bias, log_rate, skip_gain), 128
    )
    spread = spread_rows(packed)
    params = unpack_rows(spread.transpose(1, 0, 2).reshape(packed.shape[0], -1))
    all_tokens = lax.all_gather(tokens[0], "seq", axis=0, tiled=True)
    inputs = tokens[0]
    projected = jnp.dot(inputs, full_weight, preferred_element_type=jnp.float32).astype(
        jnp.bfloat16
    )
    width = projected.shape[1] // 2
    rim = K - 1
    widened = extended(projected[:, :width], (("seq", 0),), rim)
    padded = widened.astype(jnp.float32)
    gates = projected[:, width:].astype(jnp.float32)
    prepared_list = []
    prep_pulls = []
    for which in range(2):
        prepared, prep_pull = jax.vjp(
            partial(prepare, which=which),
            padded,
            params[0],
            params[1],
            params[2],
            params[3],
            params[4],
        )
        prepared_list.append(prepared)
        prep_pulls.append(prep_pull)
    gate, gate_pull = jax.vjp(jax.nn.silu, gates)
    tangent = cotangent[0].astype(jnp.float32)
    back_total = tangent * gate
    active, steps, inputs_coef, reads = (jnp.stack(pair) for pair in zip(*prepared_list))
    inputs_wide = jnp.broadcast_to(inputs_coef[..., None], inputs_coef.shape + (LANES,))
    reads_wide = jnp.broadcast_to(reads[..., None], reads.shape + (LANES,))
    rate = -jnp.exp(params[5])
    operands = (active, steps, back_total[None], inputs_wide, reads_wide, rate)
    states, flows, decays = summarise(*operands)
    told = lax.all_gather(jnp.concatenate([states, flows, decays]), "seq", axis=0)
    first = jnp.stack(
        [chain(told[:, 4], told[:, 0], False), chain(told[:, 5], told[:, 1], True)]
    )
    late = jnp.stack(
        [chain(told[:, 4], told[:, 2], True), chain(told[:, 5], told[:, 3], False)]
    )
    results = scan_all(*operands, params[6][:, None], first, late)
    outputs, active_back, steps_back, inputs_back, reads_back, rates_back, skip_back = results
    inputs_back = jnp.sum(inputs_back, axis=-1)
    reads_back = jnp.sum(reads_back, axis=-1)
    skip_back = skip_back[:, 0]
    total = outputs[0] + outputs[1]
    mixed = (total * gate).astype(jnp.bfloat16)
    back_gates = gate_pull(tangent * total)[0]
    back_padded = jnp.zeros_like(padded)
    param_backs = [jnp.zeros_like(param) for param in params[:5]]
    for which in range(2):
        more = prep_pulls[which](
            (active_back[which], steps_back[which], inputs_back[which], reads_back[which])
        )
        back_padded = back_padded + more[0]
        param_backs = [older + newer for older, newer in zip(param_backs, more[1:])]
    rims = jnp.concatenate([back_padded[:rim], back_padded[-rim:]], axis=0)
    returned = extended(rims, (("seq", 0),), rim)
    middle = back_padded[rim:-rim]
    back_values = jnp.concatenate(
        [middle[:rim] + returned[:rim], middle[rim:-rim], middle[-rim:] + returned[-rim:]], axis=0
    )
    back_projected = jnp.concatenate([back_values, back_gates], axis=1).astype(jnp.bfloat16)
    tokens_back = lax.dot_general(
        back_projected, full_weight, (((1,), (1,)), ((), ())), preferred_element_type=jnp.float32
    ).astype(jnp.bfloat16)
    groups, peers = lax.axis_size("dp"), lax.axis_size("seq")
    all_back = lax.all_gather(back_projected, "seq", axis=0, tiled=True)
    depth = all_tokens.shape[1]
    shared = all_tokens.reshape(all_tokens.shape[0], groups, peers, depth // (groups * peers))
    mine = lax.dynamic_index_in_dim(shared, lax.axis_index("seq"), 2, False)
    weight_back = lax.dot_general(
        mine.reshape(mine.shape[0], -1),
        all_back,
        (((0,), (0,)), ((), ())),
        preferred_element_type=jnp.float32,
    ).astype(jnp.bfloat16)
    wide = weight_back.shape[1]
    weight_back = weight_back.reshape(groups, -1, wide)
    own = skip_back.shape[1] // (groups * peers)
    small = pack_rows((*param_backs, rates_back, skip_back), wide // own).astype(jnp.bfloat16)
    height = small.shape[0]
    small = small.reshape(height, groups, peers, own).transpose(2, 1, 0, 3)
    small = lax.all_to_all(small.reshape(peers, groups, -1, wide), "seq", 0, 0)
    small = jnp.sum(small.astype(jnp.float32), axis=0).astype(jnp.bfloat16)
    joined = jnp.concatenate([weight_back, small], axis=1)
    joined = lax.all_to_all(joined, "dp", 0, 0)
    joined = jnp.sum(joined.astype(jnp.float32), axis=0)
    edge = weight_back.shape[1]
    sums = (joined[:edge], *unpack_rows(joined[edge:].reshape(height, own)))
    return (
        mixed[None],
        tokens_back[None],
        sums[0],
        sums[1],
        sums[2],
        sums[3],
        sums[4],
        sums[5],
        sums[6],
        sums[7],
    )


def solution(mesh):
    in_specs = (
        P("dp", "seq", None),
        P("dp", "seq", None),
        P("dp", None),
        P(None, None, "dp"),
        P(None, "dp"),
        P(None, "dp", None),
        P(None, None, "dp"),
        P(None, "dp"),
        P(None, None, "dp"),
        P(None, "dp"),
    )
    out_specs = (
        P("dp", "seq", None),
        P("dp", "seq", None),
        P(("dp", "seq"), None),
        P(None, None, ("dp", "seq")),
        P(None, ("dp", "seq")),
        P(None, ("dp", "seq"), None),
        P(None, None, ("dp", "seq")),
        P(None, ("dp", "seq")),
        P(None, None, ("dp", "seq")),
        P(None, ("dp", "seq")),
    )
    return jax.shard_map(shards, mesh=mesh, in_specs=in_specs, out_specs=out_specs, check_vma=False)
```
